256 devices in a mesh: section: 16 (over z, x_hi), dp: 16 (over x_lo, y, core).
Axes of the slice: x: 4 (x_hi: 2, x_lo: 2; x = x_hi * 2 + x_lo), y: 4, z: 8, core: 2. Of those that a mesh axis runs over, the one named last changes fastest.
Arguments:
- saved_a: bfloat16 [16, 2, 512, 5120], P('section', None, 'dp'), may hold values from -8 to 8
- saved_b: bfloat16 [16, 2, 512, 5120], P('section', None, 'dp'), may hold values from -8 to 8
- cot_a: bfloat16 [2, 512, 5120], P(None, 'dp'), may hold values from -0.125 to 0.125
- cot_b: bfloat16 [2, 512, 5120], P(None, 'dp'), may hold values from -0.125 to 0.125
- w_in: bfloat16 [16, 2, 5120, 256], P('section', None, 'dp'), may hold values from -0.01953125 to 0.01953125
- w_out: bfloat16 [16, 2, 256, 5120], P('section', None, 'dp'), may hold values from -0.078125 to 0.078125
- decay_rate: float32 [16, 2, 256], P('section'), may hold values from 0.004 to 0.4
Outputs:
- grad_w_in: float32 [16, 2, 5120, 256], P('section', None, 'dp')
- grad_w_out: float32 [16, 2, 256, 5120], P('section', None, 'dp')
The draws below stay inside these ranges and needn't reach their ends.
All inputs are finite; a program needn't handle non-finite values.
Results may differ from the reference program's by a relative error of at most 0.025.
Values may be sent and summed in bfloat16 or wider, within the bound.
No kernel may reach another device: no remote copies, remote signals or barrier semaphores. Data moves between devices by JAX's collectives and lax.ppermute only.
A program may use at most 64 MiB of HBM per device.

```python
import math
import jax
import jax.numpy as jnp
from jax import lax

D = 5120
STATE = 256
SEQ_LEN = 32
MICRO = 2
ROWS = 512
N_SECTION = 16
N_DP = 16


def with_spikes(drawn, rng, source, target, parts, factor):
    def block_of(position):
        return (jnp.arange(drawn.shape[position]) // (drawn.shape[position] // parts)).reshape((-1,) + (1,) * (drawn.ndim - 1 - position))

    one_side = jax.random.permutation(rng, parts)[block_of(target)]
    second = (block_of(target) + parts // 2) % parts
    return jnp.where((block_of(source) == one_side) | (block_of(source) == second), factor * drawn, drawn)


def block_scale(key, extent, shards, least, high):
    def one(axis_at, blocks):
        steps = jax.random.uniform(jax.random.fold_in(jax.random.fold_in(key, 6), axis_at), (blocks,), jnp.float32, least / len(shards), high / len(shards))
        return jnp.repeat(jnp.exp(steps), extent[axis_at] // blocks).reshape((-1,) + (1,) * (len(extent) - axis_at - 1))

    loudness = one(*shards[0])
    for cut in shards[1:]:
        loudness = loudness * one(*cut)
    return loudness


def noise(key, extent, width, reach, split=(), kind=jnp.bfloat16):
    values = jax.random.normal(key, extent, jnp.float32) * width
    if len(split) > 0:
        values = block_scale(key, extent, split, -0.22, 0.18) * values
    return jnp.clip(values, min=-reach, max=reach).astype(kind)


def gaussian_with(own_key, dims, width, reach, cuts, heavy, dtype=jnp.bfloat16):
    values = width * jax.random.normal(own_key, dims, jnp.float32)
    if cuts:
        values = values * block_scale(own_key, dims, cuts, -0.22, 0.18)
    return jnp.clip(with_spikes(values, jax.random.fold_in(own_key, 3), *heavy), -reach, reach).astype(dtype)


def setup_inputs(seed: int = 0) -> dict:
    key_list = jax.random.split(jax.random.key(seed), 8)
    saved_a = gaussian_with(key_list[0], (N_SECTION, MICRO, ROWS, D), 1.0, 8.0, ((0, 16), (2, 16)), (2, 3, 16, 2.0))
    saved_b = gaussian_with(key_list[1], (N_SECTION, MICRO, ROWS, D), 1.0, 8.0, ((0, 16), (2, 16)), (2, 3, 16, 2.0))
    cot_a = noise(key_list[2], (MICRO, ROWS, D), 0.02, 0.125, ((1, 16),))
    cot_b = noise(key_list[3], (MICRO, ROWS, D), 0.02, 0.125, ((1, 16),))
    w_in = noise(key_list[4], (N_SECTION, 2, D, STATE), (16 * D) ** -0.5, 0.01953125, ((0, 16), (2, 16)))
    w_out = noise(key_list[5], (N_SECTION, 2, STATE, D), D ** -0.5, 0.078125, ((0, 16), (2, 16)))
    decay_rate = jnp.clip(jnp.exp(math.log(0.4) - 4.6051702 * jax.random.uniform(key_list[6], (N_SECTION, 2, STATE), jnp.float32) ** block_scale(key_list[6], (N_SECTION, 2, STATE), ((0, 16),), -0.2, 0.2)), 0.004, 0.4)
    return dict(saved_a=saved_a, saved_b=saved_b, cot_a=cot_a, cot_b=cot_b, w_in=w_in, w_out=w_out, decay_rate=decay_rate)


def forward_states(inputs, w_input, rates):
    hidden = jnp.dot(inputs.reshape(-1, D), w_input, preferred_element_type=jnp.float32)
    hidden = hidden.reshape(MICRO, N_DP, SEQ_LEN, STATE)
    retain = jnp.exp(-rates)

    def advance(carry, current):
        carry = retain * carry + current
        return carry, carry

    start = jnp.zeros((MICRO, N_DP, STATE), jnp.float32)
    final_state, states = lax.scan(advance, start, jnp.moveaxis(hidden, 2, 0))
    return jnp.moveaxis(states, 0, 2).astype(jnp.bfloat16)


def block_backward(inputs, upstream, w_input, w_output, rates):
    latent = forward_states(inputs, w_input, rates)
    latent_grad = jnp.dot(upstream.reshape(-1, D), w_output.T, preferred_element_type=jnp.float32)
    latent_grad = latent_grad.reshape(MICRO, N_DP, SEQ_LEN, STATE)
    retain = jnp.exp(-rates)

    def retreat(carry, current):
        carry = retain * carry + current
        return carry, carry

    start = jnp.zeros((MICRO, N_DP, STATE), jnp.float32)
    final_carry, carries = lax.scan(retreat, start, jnp.moveaxis(latent_grad, 2, 0), reverse=True)
    state_grad = jnp.moveaxis(carries, 0, 2).astype(jnp.bfloat16)
    carried = jnp.dot(state_grad.reshape(-1, STATE), w_input.T, preferred_element_type=jnp.float32)
    downstream = (upstream.astype(jnp.float32) + carried.reshape(MICRO, N_DP, SEQ_LEN, D)).astype(jnp.bfloat16)
    part_in = jnp.einsum('mrtd,mrts->rds', inputs.astype(jnp.float32), state_grad.astype(jnp.float32)).astype(jnp.bfloat16)
    part_out = jnp.einsum('mrts,mrtd->rsd', latent.astype(jnp.float32), upstream.astype(jnp.float32)).astype(jnp.bfloat16)
    return downstream, jnp.sum(part_in.astype(jnp.float32), axis=0), jnp.sum(part_out.astype(jnp.float32), axis=0)


def shape_rows(array):
    return array.reshape(MICRO, N_DP, SEQ_LEN, D)


def section_pass(upstream, pieces):
    inputs, w_input, w_output, rates = pieces
    downstream, grad_input, grad_output = block_backward(shape_rows(inputs), upstream, w_input, w_output, rates)
    return downstream, (grad_input, grad_output)


def reference(saved_a, saved_b, cot_a, cot_b, w_in, w_out, decay_rate):
    final_down, grads_down = lax.scan(section_pass, shape_rows(cot_a), (saved_a, w_in[:, 0], w_out[:, 0], decay_rate[:, 0]), reverse=True)
    final_up, grads_up = lax.scan(section_pass, shape_rows(cot_b), (saved_b, w_in[:, 1], w_out[:, 1], decay_rate[:, 1]))
    grad_w_in = jnp.stack([grads_down[0], grads_up[0]], axis=1)
    grad_w_out = jnp.stack([grads_down[1], grads_up[1]], axis=1)
    return grad_w_in, grad_w_out
```

```python
import functools

import jax
import jax.numpy as jnp
from jax import lax
from jax.experimental import pallas as pl
from jax.experimental.pallas import tpu as pltpu
from jax.sharding import Mesh, PartitionSpec as P

SECTION = ("z", "xh")
CHIPS = ("xl", "y")
DP = ("xl", "y", "core")
PLANES = 8
SEQ = 32
SWAP = [(0, 1), (1, 0)]
BF, F32 = jnp.bfloat16, jnp.float32


def swap(block, axis):
    return lax.ppermute(block, axis, SWAP)


def dot(a, b, contract):
    return lax.dot_general(a, b, (contract, ((), ())), preferred_element_type=F32)


def time_scan(values, rates, reverse):
    rows = values.shape[0]
    place = lax.broadcasted_iota(jnp.int32, values.shape, 0) % SEQ
    for step in (1, 2, 4, 8, 16):
        if reverse:
            moved = pltpu.roll(values, rows - step, 0)
            inside = place < SEQ - step
        else:
            moved = pltpu.roll(values, step, 0)
            inside = place >= step
        values = values + jnp.where(inside, moved, 0.0) * jnp.exp(-rates * step)
    return values


def relay_kernel(mine, other, u_ref, m_ref, rates_ref, w_hbm, sg_ref, u1_ref, u2_ref, w_vmem, sems):
    copies = [
        pltpu.make_async_copy(w_hbm.at[i], w_vmem.at[i], sems.at[i]) for i in range(2)
    ]
    for copy in copies:
        copy.start()
    state = m_ref.shape[0]
    grad = mine[...] + other[...]
    first = time_scan(grad[:, :state], rates_ref[0:1, :], True).astype(BF)
    sg_ref[0] = first
    grad2 = grad[:, state:] + dot(first, m_ref[...], ((1,), (0,)))
    second = time_scan(grad2, rates_ref[1:2, :], True).astype(BF)
    sg_ref[1] = second
    width = u_ref.shape[1]
    tile = 512
    copies[0].wait()
    for at in range(0, width, tile):
        cols = pl.ds(at, tile)
        carried = dot(first, w_vmem[0, cols, :], ((1,), (1,)))
        u1_ref[:, cols] = (u_ref[:, cols].astype(F32) + carried).astype(BF)
    copies[1].wait()
    for at in range(0, width, tile):
        cols = pl.ds(at, tile)
        carried = dot(second, w_vmem[1, cols, :], ((1,), (1,)))
        u2_ref[:, cols] = (u1_ref[:, cols].astype(F32) + carried).astype(BF)


def relay_step(mine, other, upstream, between, rates, w_input):
    rows, width = upstream.shape
    state = between.shape[0]
    vmem = pl.BlockSpec(memory_space=pltpu.VMEM)
    return pl.pallas_call(
        relay_kernel,
        out_shape=(
            jax.ShapeDtypeStruct((2, rows, state), BF),
            jax.ShapeDtypeStruct((rows, width), BF),
            jax.ShapeDtypeStruct((rows, width), BF),
        ),
        in_specs=[vmem] * 5 + [pl.BlockSpec(memory_space=pl.ANY)],
        out_specs=(vmem, vmem, vmem),
        scratch_shapes=[
            pltpu.VMEM((2, width, state), BF),
            pltpu.SemaphoreType.DMA((2,)),
        ],
        compiler_params=pltpu.CompilerParams(vmem_limit_bytes=16 * 2**20),
        cost_estimate=pl.CostEstimate(
            flops=4 * rows * width * state, bytes_accessed=4 * width * state, transcendentals=0
        ),
    )(mine, other, upstream, between, rates, w_input)


def latent_kernel(mine, other, rates_ref, out_ref):
    for place in range(2):
        hidden = mine[place] + other[place]
        out_ref[place] = time_scan(hidden, rates_ref[place : place + 1, :], False).astype(BF)


def latents(mine, other, rates):
    vmem = pl.BlockSpec(memory_space=pltpu.VMEM)
    return pl.pallas_call(
        latent_kernel,
        out_shape=jax.ShapeDtypeStruct(mine.shape, BF),
        in_specs=[vmem] * 3,
        out_specs=vmem,
        compiler_params=pltpu.CompilerParams(vmem_limit_bytes=16 * 2**20),
    )(mine, other, rates)


def on_device(saved_a, saved_b, cot_a, cot_b, w_in, w_out, decay_rate):
    plane, half, core = lax.axis_index("z"), lax.axis_index("xh"), lax.axis_index("core")
    chips = lax.axis_size(CHIPS)
    micro, length, width = saved_a.shape[1:]
    part = width // (2 * chips)
    state = w_in.shape[3]

    def by_half(a, b):
        return jnp.where(half == 0, a, b)

    def by_core(a, b):
        return jnp.where(core == 0, a, b)

    def columns(block):
        even = jnp.concatenate(
            [block[..., 2 * i * part : (2 * i + 1) * part] for i in range(chips)], axis=-1
        )
        odd = jnp.concatenate(
            [block[..., (2 * i + 1) * part : (2 * i + 2) * part] for i in range(chips)], axis=-1
        )
        return by_core(even, odd), by_core(odd, even)

    def pair_rows(block, axis):
        keep, give = columns(block)
        got = swap(give, "core")
        return by_core(
            jnp.concatenate([keep, got], axis=axis), jnp.concatenate([got, keep], axis=axis)
        )

    def both_places(own_a, own_b):
        return jnp.stack([swap(by_half(own_b, own_a), "xh"), by_half(own_a, own_b)])

    shard_in = both_places(w_in[0, 0], w_in[0, 1])
    shard_out = pair_rows(both_places(w_out[0, 0], w_out[0, 1]), 1)
    rates = both_places(decay_rate[0, 0], decay_rate[0, 1])
    weights_out = lax.all_gather(shard_out, CHIPS, axis=1, tiled=True)
    weights_in = lax.all_gather(shard_in, CHIPS, axis=1, tiled=True)

    cot = pair_rows(by_half(cot_a, cot_b), 1)
    rows = cot.shape[1]
    inputs = pair_rows(both_places(saved_a[0], saved_b[0]), 2)

    between = dot(weights_in[0], weights_out[1], ((0,), (1,)))
    between = (between + swap(between, "core")).astype(BF)
    weights_out = weights_out.reshape(2 * state, width // 2)

    place = by_half(PLANES - 1 - plane, plane)
    uppers = jnp.zeros((micro + 1, 2, rows, width // 2), BF)
    states = jnp.zeros((micro + 1, 2, rows, state), BF)
    incoming = cot[0]
    steps = PLANES + micro - 1
    for step in range(steps):
        if 0 < step < micro:
            incoming = jnp.where(place == 0, cot[step], incoming)
        mine = dot(incoming, weights_out, ((1,), (1,)))
        state_grad, middle, passing = relay_step(
            mine, swap(mine, "core"), incoming, between, rates, weights_in
        )
        order = step - place
        slot = jnp.where((order >= 0) & (order < micro), order, micro)
        uppers = lax.dynamic_update_slice(uppers, incoming[None, None], (slot, 0, 0, 0))
        uppers = lax.dynamic_update_slice(uppers, middle[None, None], (slot, 1, 0, 0))
        states = lax.dynamic_update_slice(states, state_grad[None], (slot, 0, 0, 0))
        if step < steps - 1:
            route = []
            for at in range(PLANES - 1):
                if 0 <= step - at < micro:
                    route.append(((PLANES - 1 - at) * 2, (PLANES - 2 - at) * 2))
                    route.append((at * 2 + 1, (at + 1) * 2 + 1))
            incoming = lax.ppermute(passing, SECTION, route)

    def cut(block):
        return jnp.stack([block[..., i * part : (i + 1) * part] for i in range(chips)])

    def own_rows(block):
        return by_core(block[..., :length, :], block[..., length:, :])

    def all_rows(got):
        other = swap(got, "core")
        return by_core(
            jnp.concatenate([got, other], axis=-2), jnp.concatenate([other, got], axis=-2)
        )

    hidden = lax.dot_general(
        inputs.reshape(2, micro * rows, width // 2),
        weights_in,
        (((2,), (1,)), ((0,), (0,))),
        preferred_element_type=F32,
    )
    latent = latents(hidden, swap(hidden, "core"), rates).reshape(2, micro, rows, state)
    inputs_all = lax.all_to_all(cut(inputs), CHIPS, 0, 0)
    latent_own = own_rows(latent)
    latent_all = all_rows(
        lax.all_to_all(
            jnp.broadcast_to(latent_own[None], (chips,) + latent_own.shape), CHIPS, 0, 0
        )
    )

    states_own = own_rows(states[:micro])
    uppers_all = lax.all_to_all(cut(uppers[:micro]), CHIPS, 0, 0)
    states_all = all_rows(
        lax.all_to_all(
            jnp.broadcast_to(states_own[None], (chips,) + states_own.shape), CHIPS, 0, 0
        )
    )
    grad_in = jnp.stack(
        [
            dot(inputs_all[:, p], states_all[:, :, p], ((0, 1, 2), (0, 1, 2))).astype(BF)
            for p in range(2)
        ]
    )
    grad_out = jnp.stack(
        [
            dot(latent_all[:, p], uppers_all[:, :, p], ((0, 1, 2), (0, 1, 2))).astype(BF)
            for p in range(2)
        ]
    )
    pieces = grad_out.reshape(2, 2 * chips, state // (2 * chips), part).transpose(1, 0, 2, 3)
    pieces = lax.all_to_all(pieces, DP, 0, 0)
    grad_out = pieces.transpose(1, 2, 0, 3).reshape(2, state // (2 * chips), width)

    def home(both):
        other = swap(both[0], "xh").astype(F32)
        own = both[1].astype(F32)
        return jnp.stack([by_half(own, other), by_half(other, own)])[None]

    return home(grad_in), home(grad_out)


def solution(mesh):
    parts = Mesh(mesh.devices.reshape(PLANES, 2, 2, 4, 2), ("z", "xh", "xl", "y", "core"))
    rows = P(SECTION, None, DP, None)
    return jax.shard_map(
        on_device,
        mesh=parts,
        in_specs=(
            rows,
            rows,
            P(None, DP, None),
            P(None, DP, None),
            rows,
            rows,
            P(SECTION, None, None),
        ),
        out_specs=(rows, rows),
        check_vma=False,
    )
```

```python
import jax
import jax.numpy as jnp
from jax import lax
from jax.experimental import pallas as pl
from jax.experimental.pallas import tpu as pltpu
from jax.sharding import Mesh, PartitionSpec as P

SECTION = ("z", "xh")
CHIPS = ("xl", "y")
DP = ("xl", "y", "core")
PLANES = 8
SEQ = 32
CHUNKS = 4
SKEW = 2
SWAP = [(0, 1), (1, 0)]
BF, F32 = jnp.bfloat16, jnp.float32
SHORT = pl.CostEstimate(flops=1, bytes_accessed=1, transcendentals=0)
VMEM = pl.BlockSpec(memory_space=pltpu.VMEM)
SMEM = pl.BlockSpec(memory_space=pltpu.SMEM)
ANY = pl.BlockSpec(memory_space=pl.ANY)


def swap(block, axis):
    return lax.ppermute(block, axis, SWAP)


def dot(a, b, contract):
    return lax.dot_general(a, b, (contract, ((), ())), preferred_element_type=F32)


def params(mib):
    return pltpu.CompilerParams(vmem_limit_bytes=mib * 2**20)


def lanes(count):
    return -(-count // 128) * 128


def time_scan(values, rates, reverse):
    rows = values.shape[0]
    place = lax.broadcasted_iota(jnp.int32, values.shape, 0) % SEQ
    for step in (1, 2, 4, 8, 16):
        if reverse:
            moved = pltpu.roll(values, rows - step, 0)
            inside = place < SEQ - step
        else:
            moved = pltpu.roll(values, step, 0)
            inside = place >= step
        values = values + jnp.where(inside, moved, 0.0) * jnp.exp(-rates * step)
    return values


NEAR = ((0, 0), (0, 1), (0, 3), (1, 0), (0, 2), (1, 1), (1, 3), (1, 2))


def unpack_kernel(*refs):
    chips = len(NEAR)
    blocks, (w_in_ref, w_out_ref, between_ref, rest, sems) = refs[: 2 * chips], refs[2 * chips :]
    depth, state = rest.shape[1:]
    share = state // chips
    xl, y = lax.axis_index("xl"), lax.axis_index("y")
    near = [lax.rem(xl + over, 2) * 4 + lax.rem(y + up, 4) for over, up in NEAR]
    copies = []
    for n, block in enumerate(blocks):
        at = pl.multiple_of(near[n % chips] * depth, depth)
        copies.append(
            (
                pltpu.make_async_copy(block.at[pl.ds(depth, depth)], rest.at[n], sems.at[n, 0]),
                pltpu.make_async_copy(
                    block.at[pl.ds(0, depth)],
                    w_in_ref.at[n // chips, pl.ds(at, depth)],
                    sems.at[n, 1],
                ),
            )
        )
        for copy in copies[n]:
            copy.start()
    for n in range(len(blocks)):
        for copy in copies[n]:
            copy.wait()
        at = pl.multiple_of(n // chips * state + near[n % chips] * share, share)
        for t in range(depth // share):
            w_out_ref[pl.ds(at, share), t * state : (t + 1) * state] = rest[
                n, t * share : (t + 1) * share, :
            ]
    between_ref[...] = dot(w_in_ref[0], w_out_ref[state:, :], ((0,), (1,)))


def unpack(blocks):
    chips = len(NEAR)
    depth, state = blocks[0].shape[0] // 2, blocks[0].shape[1]
    return pl.pallas_call(
        unpack_kernel,
        out_shape=(
            jax.ShapeDtypeStruct((2, chips * depth, state), BF),
            jax.ShapeDtypeStruct((2 * state, chips * depth), BF),
            jax.ShapeDtypeStruct((state, state), F32),
        ),
        in_specs=[ANY] * len(blocks),
        out_specs=(VMEM,) * 3,
        scratch_shapes=[
            pltpu.VMEM((len(blocks), depth, state), BF),
            pltpu.SemaphoreType.DMA((len(blocks), 2)),
        ],
        cost_estimate=SHORT,
        compiler_params=params(16),
    )(*blocks)


def gather_blocks(own, first):
    def hop(block, over, up):
        route = [
            (x * 4 + y, (x + over) % 2 * 4 + (y - up) % 4) for x in range(2) for y in range(4)
        ]
        return lax.ppermute(block, CHIPS, route)

    near = {}
    for name, block in (("own", own), ("first", first)):
        near[name] = {(0, 0): block}
        for over, up in ((0, 1), (0, 3), (1, 0)):
            near[name][over, up] = hop(block, over, up)
    o, f = near["own"], near["first"]
    o[0, 2] = hop(o[0, 1], 0, 1)
    f[0, 2] = hop(f[0, 3], 0, 3)
    o[1, 3] = hop(o[0, 3], 1, 0)
    o[1, 1] = hop(o[1, 0], 0, 1)
    f[1, 3] = hop(f[1, 0], 0, 3)
    f[1, 1] = hop(f[0, 1], 1, 0)
    o[1, 2] = hop(o[1, 1], 0, 1)
    f[1, 2] = hop(f[1, 3], 0, 3)
    return [f[at] for at in NEAR] + [o[at] for at in NEAR]


TOKEN = jax.ShapeDtypeStruct((8, 128), F32)


def working(step):
    half, plane = lax.axis_index("xh"), lax.axis_index("z")
    order = step - SKEW * jnp.where(half == 0, PLANES - 1 - plane, plane)
    return (order >= 0) & (order < CHUNKS)


def project_kernel(step, u_ref, w_ref, *refs):
    out_ref = refs[-1]

    @pl.when(working(step))
    def _():
        out_ref[...] = dot(u_ref[...], w_ref[...], ((1,), (1,)))


def project_start_kernel(step, u_ref, chunk_ref, w_ref, *refs):
    out_ref, used_ref = refs[-2:]
    half, plane = lax.axis_index("xh"), lax.axis_index("z")
    place = jnp.where(half == 0, PLANES - 1 - plane, plane)

    @pl.when(place == 0)
    def _():
        used_ref[...] = chunk_ref[...]

    @pl.when(place != 0)
    def _():
        used_ref[...] = u_ref[...]

    @pl.when(working(step))
    def _():
        out_ref[...] = dot(used_ref[...], w_ref[...], ((1,), (1,)))


def project(step, upstream, chunk, weights_out, tokens):
    if upstream is None:
        upstream, chunk = chunk, None
    rows, width = upstream.shape
    double = weights_out.shape[0]
    kernel, given = project_kernel, (upstream,)
    out = (jax.ShapeDtypeStruct((rows, double), F32),)
    if chunk is not None:
        kernel, given = project_start_kernel, (upstream, chunk)
        out += (jax.ShapeDtypeStruct((rows, width), BF),)
    found = pl.pallas_call(
        lambda *refs: kernel(step, *refs),
        out_shape=out,
        in_specs=[VMEM] * (len(given) + 1 + len(tokens)),
        out_specs=(VMEM,) * len(out),
        cost_estimate=SHORT,
        compiler_params=params(8),
    )(*given, weights_out, *tokens)
    return (found[0], upstream) if chunk is None else found


def relay_kernel(
    step, mine, other, u_ref, m_ref, rates_ref, w_ref, sg_hbm, u2_ref, token, sg, sem
):
    del token
    @pl.when(working(step))
    def _():
        state = m_ref.shape[0]
        grad = mine[...] + other[...]
        first = time_scan(grad[:, :state], rates_ref[0:1, :], True).astype(BF)
        sg[0] = first
        grad2 = grad[:, state:] + dot(first, m_ref[...], ((1,), (0,)))
        second = time_scan(grad2, rates_ref[1:2, :], True).astype(BF)
        sg[1] = second
        copy = pltpu.make_async_copy(sg, sg_hbm, sem)
        copy.start()
        width = u_ref.shape[1]
        tile = 512
        for at in range(0, width, tile):
            cols = pl.ds(at, tile)
            carried = dot(first, w_ref[0, cols, :], ((1,), (1,)))
            middle = (u_ref[:, cols].astype(F32) + carried).astype(BF)
            carried = dot(second, w_ref[1, cols, :], ((1,), (1,)))
            u2_ref[:, cols] = (middle.astype(F32) + carried).astype(BF)
        copy.wait()


def relay_step(step, mine, other, upstream, between, rates, weights_in):
    rows, width = upstream.shape
    state = between.shape[0]
    return pl.pallas_call(
        lambda *refs: relay_kernel(step, *refs),
        out_shape=(
            jax.ShapeDtypeStruct((2, rows, state), BF),
            jax.ShapeDtypeStruct((rows, width), BF),
            TOKEN,
        ),
        in_specs=[VMEM] * 6,
        out_specs=(ANY, VMEM, VMEM),
        scratch_shapes=[pltpu.VMEM((2, rows, state), BF), pltpu.SemaphoreType.DMA],
        cost_estimate=SHORT,
        compiler_params=params(8),
    )(mine, other, upstream, between, rates, weights_in)


def halves_kernel(spot, first, second, keep_ref, give_ref):
    part = first.shape[1] // (2 * len(NEAR))
    for place, ref in enumerate((first, second)):
        for i in range(len(NEAR)):
            even = ref[:, 2 * i * part : (2 * i + 1) * part]
            odd = ref[:, (2 * i + 1) * part : (2 * i + 2) * part]
            own = spot[1] == 0
            keep_ref[place, :, i * part : (i + 1) * part] = jnp.where(own, even, odd)
            give_ref[place, :, i * part : (i + 1) * part] = jnp.where(own, odd, even)


def halves(spot, first, second):
    rows, width = first.shape
    return pl.pallas_call(
        halves_kernel,
        out_shape=(jax.ShapeDtypeStruct((2, rows, width // 2), BF),) * 2,
        in_specs=[SMEM, VMEM, VMEM],
        out_specs=(VMEM,) * 2,
        cost_estimate=SHORT,
        compiler_params=params(16),
    )(spot, first, second)


def cut_kernel(first, second, cut_ref, token):
    del token
    count, _, _, part = cut_ref.shape
    for place, ref in enumerate((first, second)):
        for j in range(count):
            cut_ref[j, place] = ref[:, j * part : (j + 1) * part]


def cut_saved(first, second, count):
    rows, width = first.shape
    return pl.pallas_call(
        cut_kernel,
        out_shape=(jax.ShapeDtypeStruct((count, 2, rows, width // count), BF), TOKEN),
        in_specs=[VMEM, VMEM],
        out_specs=(VMEM,) * 2,
        cost_estimate=SHORT,
        compiler_params=params(16),
    )(first, second)


def hidden_kernel(keep, got, w_ref, behind, mine_ref, other_ref):
    del behind
    for place in range(2):
        mine_ref[place] = dot(keep[place], w_ref[place], ((1,), (0,)))
        other_ref[place] = dot(got[place], w_ref[place], ((1,), (0,)))


def hidden_parts(keep, got, weights_in, behind):
    _, rows, _ = keep.shape
    return pl.pallas_call(
        hidden_kernel,
        out_shape=(jax.ShapeDtypeStruct((2, rows, weights_in.shape[2]), F32),) * 2,
        in_specs=[VMEM] * 4,
        out_specs=(VMEM,) * 2,
        cost_estimate=SHORT,
        compiler_params=params(8),
    )(keep, got, weights_in, behind)


def latent_kernel(mine, other, rates_ref, out_ref):
    for place in range(2):
        hidden = mine[place] + other[place]
        latent = time_scan(hidden, rates_ref[place : place + 1, :], False).astype(BF)
        for i in range(out_ref.shape[0]):
            out_ref[i, place] = latent


def latents(mine, other, rates, chips):
    return pl.pallas_call(
        latent_kernel,
        out_shape=jax.ShapeDtypeStruct((chips,) + mine.shape, BF),
        in_specs=[VMEM] * 3,
        out_specs=VMEM,
        cost_estimate=SHORT,
        compiler_params=params(8),
    )(mine, other, rates)


def collect_kernel(steps, spot, *refs):
    uppers, states = refs[:steps], refs[steps : 2 * steps]
    out_ref, _, upper, state, sems = refs[2 * steps :]
    chunks = CHUNKS
    chips, _, _, wide = out_ref.shape
    part = upper.shape[2] // chips
    width = state.shape[3]
    for t in range(PLANES):

        @pl.when(spot[2] == t)
        def _():
            copies = []
            for n in range(chunks):
                at = SKEW * t + n
                copies.append(pltpu.make_async_copy(uppers[at], upper.at[n], sems.at[n]))
                copies.append(pltpu.make_async_copy(states[at], state.at[n], sems.at[chunks + n]))
            for copy in copies:
                copy.start()
            for copy in copies:
                copy.wait()

    for n in range(chunks):
        own = state[2 * (n // 2) + spot[1], n % 2]
        for i in range(chips):
            out_ref[i, n, :, :part] = upper[n, :, i * part : (i + 1) * part]
            out_ref[i, n, :, wide - width :] = own


def collect(spot, uppers, states, chips):
    steps, chunks = len(uppers), CHUNKS
    rows, width = uppers[0].shape
    state = states[0].shape[2]
    wide = lanes(width // chips) + state
    return pl.pallas_call(
        lambda *refs: collect_kernel(steps, *refs),
        out_shape=(jax.ShapeDtypeStruct((chips, chunks, rows, wide), BF), TOKEN),
        in_specs=[SMEM] + [ANY] * (2 * steps),
        out_specs=(VMEM,) * 2,
        scratch_shapes=[
            pltpu.VMEM((chunks, rows, width), BF),
            pltpu.VMEM((chunks, 2, rows, state), BF),
            pltpu.SemaphoreType.DMA((2 * chunks,)),
        ],
        cost_estimate=SHORT,
        compiler_params=params(16),
    )(spot, *uppers, *states)


def gradient_kernel(
    spot, x_ref, lat_own, lat_other, relayed, sg_other, w_ref, in_ref, out_ref, sum_in, sum_out
):
    part, state = in_ref.shape[1:]
    wide = relayed.shape[-1]
    group = relayed.shape[0]
    turn = pl.program_id(0)

    @pl.when(turn == 0)
    def _():
        sum_in[...] = jnp.zeros_like(sum_in)
        sum_out[...] = jnp.zeros_like(sum_out)

    def by_core(own, other):
        even = jnp.where(spot[1] == 0, own, other)
        odd = jnp.where(spot[1] == 0, other, own)
        return jnp.stack([even, odd], axis=1)

    micro = relayed.shape[1] // 2
    mine = relayed[:, :, :, wide - state :]
    theirs = sg_other[...]
    upper = relayed[:, :, :, :part]
    upper = jnp.stack(
        [jnp.stack([upper[:, 2 * m + r] for m in range(micro)], axis=1) for r in range(2)], axis=1
    ).reshape(-1, part)
    for place in range(2):
        grad = by_core(
            jnp.stack([mine[:, 2 * m + place] for m in range(micro)], axis=1),
            jnp.stack([theirs[:, 2 * m + place] for m in range(micro)], axis=1),
        ).reshape(-1, state)
        latent = by_core(lat_own[:, place], lat_other[:, place]).reshape(-1, state)
        x = x_ref[:, place].reshape(-1, part)
        sum_in[place] += dot(x, grad, ((0,), (0,)))
        sum_out[place] += dot(latent, upper, ((0,), (0,)))
        if place == 0:
            carried = dot(grad, w_ref[...], ((1,), (1,)))
            upper = (upper.astype(F32) + carried).astype(BF)

    @pl.when(turn == pl.num_programs(0) - 1)
    def _():
        in_ref[...] = sum_in[...].astype(BF)
        out_ref[spot[0]] = sum_out[1].astype(BF)
        out_ref[1 - spot[0]] = sum_out[0].astype(BF)


def gradients(spot, x_all, lat_own, lat_other, relayed, sg_other, weight):
    chips, chunks, rows, wide = relayed.shape
    part, state = weight.shape
    group = 2

    def blocks(array, count):
        rest = array.shape[1:]
        return pl.BlockSpec((count,) + rest, lambda i: (i,) + (0,) * len(rest))

    return pl.pallas_call(
        gradient_kernel,
        grid=(chips // group,),
        out_shape=(
            jax.ShapeDtypeStruct((2, part, state), BF),
            jax.ShapeDtypeStruct((2, state, part), BF),
        ),
        in_specs=[
            SMEM,
            blocks(x_all, 2 * group),
            blocks(lat_own, group),
            blocks(lat_other, group),
            blocks(relayed, group),
            blocks(sg_other, group),
            pl.BlockSpec(weight.shape, lambda i: (0, 0)),
        ],
        out_specs=(
            pl.BlockSpec((2, part, state), lambda i: (0, 0, 0)),
            pl.BlockSpec((2, state, part), lambda i: (0, 0, 0)),
        ),
        scratch_shapes=[pltpu.VMEM((2, part, state), F32), pltpu.VMEM((2, state, part), F32)],
        cost_estimate=SHORT,
        compiler_params=params(24),
    )(spot, x_all, lat_own, lat_other, relayed, sg_other, weight)


def on_device(saved_a, saved_b, cot_a, cot_b, w_in, w_out, decay_rate):
    plane, half, core = lax.axis_index("z"), lax.axis_index("xh"), lax.axis_index("core")
    chips = lax.axis_size(CHIPS)
    micro, length, width = saved_a.shape[1:]
    part = width // (2 * chips)
    state = w_in.shape[3]
    share = state // chips
    chunks = 2 * micro
    place = jnp.where(half == 0, PLANES - 1 - plane, plane)
    spot = jnp.stack([half, core, place]).astype(jnp.int32)

    def by_half(a, b):
        return jnp.where(half == 0, a, b)

    def by_core(a, b):
        return jnp.where(core == 0, a, b)

    def pair_rows(block, axis):
        even = jnp.concatenate(
            [block[..., 2 * i * part : (2 * i + 1) * part] for i in range(chips)], axis=-1
        )
        odd = jnp.concatenate(
            [block[..., (2 * i + 1) * part : (2 * i + 2) * part] for i in range(chips)], axis=-1
        )
        keep, got = by_core(even, odd), swap(by_core(odd, even), "core")
        return by_core(
            jnp.concatenate([keep, got], axis=axis), jnp.concatenate([got, keep], axis=axis)
        )

    shard_out = pair_rows(w_out[0], 1).reshape(2, share, width // (2 * state), state)
    shard_out = shard_out.transpose(0, 2, 1, 3).reshape(2, part, state)
    shard = jnp.concatenate([w_in[0], shard_out], axis=1)
    own = by_half(shard[0], shard[1])
    first = swap(by_half(shard[1], shard[0]), "xh")
    first_rate = swap(by_half(decay_rate[0, 1], decay_rate[0, 0]), "xh")
    rates = jnp.stack([first_rate, by_half(decay_rate[0, 0], decay_rate[0, 1])])

    weights_in, weights_out, between = unpack(gather_blocks(own, first))
    cot = pair_rows(by_half(cot_a, cot_b), 1).reshape(chunks, length, width // 2)
    between = (between + swap(between, "core")).astype(BF)
    saved_own = by_half(saved_a[0], saved_b[0]).reshape(micro * length, width)
    saved_first = swap(by_half(saved_b[0], saved_a[0]), "xh").reshape(micro * length, width)
    cut, cut_done = cut_saved(saved_first, saved_own, 2 * chips)
    x_all = lax.all_to_all(cut, DP, 0, 0)
    keep, give = halves(spot, saved_first, saved_own)
    got = swap(give, "core")

    steps = SKEW * (PLANES - 1) + chunks
    arriving, uppers, states = {}, [], []
    tokens = (cut_done, got[0, :8, :128])
    for step in range(steps):
        chunk = cot[step] if step < chunks else None
        part_grad, upstream = project(step, arriving.get(step), chunk, weights_out, tokens)
        state_grad, passing, token = relay_step(
            step, part_grad, swap(part_grad, "core"), upstream, between, rates, weights_in
        )
        uppers.append(upstream)
        states.append(state_grad)
        tokens = (token,)
        if step == 8:
            tokens += (x_all[0, 0, :8, :128],)
        route = []
        for at in range(PLANES - 1):
            if 0 <= step - SKEW * at < chunks:
                route.append(((PLANES - 1 - at) * 2, (PLANES - 2 - at) * 2))
                route.append((at * 2 + 1, (at + 1) * 2 + 1))
        if route:
            arriving[step + SKEW] = lax.ppermute(passing, SECTION, route)

    relayed, token = collect(spot, uppers, states, chips)
    relayed = lax.all_to_all(relayed, CHIPS, 0, 0)
    mine, other = hidden_parts(keep, got, weights_in, token)
    latent = latents(mine, swap(other, "core"), rates, chips)
    latent_all = lax.all_to_all(latent, CHIPS, 0, 0)
    latent_other = swap(latent_all, "core")
    sg_other = swap(relayed[..., lanes(part) :], "core")
    grad_in, grad_out = gradients(spot, x_all, latent_all, latent_other, relayed, sg_other, first[:part])
    other_in = swap(grad_in[0], "xh")
    grad_in = jnp.stack([by_half(grad_in[1], other_in), by_half(other_in, grad_in[1])])
    rows = state // (2 * chips)
    grad_out = lax.all_to_all(grad_out.reshape(4 * chips, rows, part), ("xh",) + DP, 0, 0)
    grad_out = grad_out.reshape(2, 2 * chips, rows, part).transpose(0, 2, 1, 3)
    grad_out = grad_out.reshape(2, rows, width)
    return grad_in.astype(F32)[None], grad_out.astype(F32)[None]


def solution(mesh):
    parts = Mesh(mesh.devices.reshape(PLANES, 2, 2, 4, 2), ("z", "xh", "xl", "y", "core"))
    rows = P(SECTION, None, DP, None)
    return jax.shard_map(
        on_device,
        mesh=parts,
        in_specs=(
            rows,
            rows,
            P(None, DP, None),
            P(None, DP, None),
            rows,
            rows,
            P(SECTION, None, None),
        ),
        out_specs=(rows, rows),
        check_vma=False,
    )
```

```python
import jax
import jax.numpy as jnp
from jax import lax
from jax.experimental import pallas as pl
from jax.experimental.pallas import tpu as pltpu
from jax.sharding import Mesh, PartitionSpec as P

SECTION = ("z", "xh")
CHIPS = ("xl", "y")
DP = ("xl", "y", "core")
PLANES = 8
SEQ = 32
CHUNKS = 4
SKEW = 2
SWAP = [(0, 1), (1, 0)]
BF, F32 = jnp.bfloat16, jnp.float32
SHORT = pl.CostEstimate(flops=1, bytes_accessed=1, transcendentals=0)
TOKEN = jax.ShapeDtypeStruct((8, 128), F32)
VMEM = pl.BlockSpec(memory_space=pltpu.VMEM)
SMEM = pl.BlockSpec(memory_space=pltpu.SMEM)
ANY = pl.BlockSpec(memory_space=pl.ANY)


def swap(block, axis):
    return lax.ppermute(block, axis, SWAP)


def dot(a, b, contract):
    return lax.dot_general(a, b, (contract, ((), ())), preferred_element_type=F32)


def params(mib):
    return pltpu.CompilerParams(vmem_limit_bytes=mib * 2**20)


def lanes(count):
    return -(-count // 128) * 128


def time_scan(values, rates, reverse):
    rows = values.shape[0]
    place = lax.broadcasted_iota(jnp.int32, values.shape, 0) % SEQ
    for step in (1, 2, 4, 8, 16):
        if reverse:
            moved = pltpu.roll(values, rows - step, 0)
            inside = place < SEQ - step
        else:
            moved = pltpu.roll(values, step, 0)
            inside = place >= step
        values = values + jnp.where(inside, moved, 0.0) * jnp.exp(-rates * step)
    return values


NEAR = ((0, 0), (0, 1), (0, 3), (1, 0), (0, 2), (1, 1), (1, 3), (1, 2))


def place_blocks(spots, blocks, w_in_ref, w_out_ref):
    depth, state = blocks[0].shape[0] // 2, blocks[0].shape[1]
    share = state // len(NEAR)
    xl, y = lax.axis_index("xl"), lax.axis_index("y")
    for (place, (over, up)), packed in zip(spots, blocks):
        i = lax.rem(xl + over, 2) * 4 + lax.rem(y + up, 4)
        at = pl.multiple_of(i * depth, depth)
        w_in_ref[place, pl.ds(at, depth), :] = packed[:depth, :]
        at = pl.multiple_of(place * state + i * share, share)
        for t in range(depth // share):
            w_out_ref[pl.ds(at, share), t * state : (t + 1) * state] = packed[
                depth + t * share : depth + (t + 1) * share, :
            ]


def place_first_kernel(spots, refs):
    blocks, passed = refs[: len(spots)], refs[len(spots) :][:2]
    w_in_ref, w_out_ref, *out = refs[len(spots) + 2 :]
    for block, ref in zip(passed, out):
        ref[...] = block[...]
    place_blocks(spots, blocks, w_in_ref, w_out_ref)


def place_first(spots, blocks, passed):
    depth, state = blocks[0].shape[0] // 2, blocks[0].shape[1]
    width = len(NEAR) * depth
    return pl.pallas_call(
        lambda *refs: place_first_kernel(spots, refs),
        out_shape=(
            jax.ShapeDtypeStruct((2, width, state), BF),
            jax.ShapeDtypeStruct((2 * state, width), BF),
        )
        + tuple(jax.ShapeDtypeStruct(block.shape, BF) for block in passed),
        in_specs=[VMEM] * (len(blocks) + 2),
        out_specs=(VMEM,) * 4,
        cost_estimate=SHORT,
        compiler_params=params(8),
    )(*blocks, *passed)


def place_last_kernel(spots, refs):
    blocks, (w_in_ref, w_out_ref, between_ref) = refs[: len(spots)], refs[-3:]
    place_blocks(spots, blocks, w_in_ref, w_out_ref)
    state = between_ref.shape[0]
    between_ref[...] = dot(w_in_ref[0], w_out_ref[state:, :], ((0,), (1,)))


def place_last(spots, blocks, token, weights_in, weights_out):
    state = weights_in.shape[2]
    count = len(blocks) + 1
    return pl.pallas_call(
        lambda *refs: place_last_kernel(spots, refs),
        out_shape=(
            jax.ShapeDtypeStruct(weights_in.shape, BF),
            jax.ShapeDtypeStruct(weights_out.shape, BF),
            jax.ShapeDtypeStruct((state, state), F32),
        ),
        in_specs=[VMEM] * (count + 2),
        out_specs=(VMEM,) * 3,
        input_output_aliases={count: 0, count + 1: 1},
        cost_estimate=SHORT,
        compiler_params=params(8),
    )(*blocks, token, weights_in, weights_out)


def gather_blocks(own, first, token):
    def hop(block, over, up):
        route = [
            (x * 4 + y, (x + over) % 2 * 4 + (y - up) % 4) for x in range(2) for y in range(4)
        ]
        return lax.ppermute(block, CHIPS, route)

    o, f = {(0, 0): own}, {(0, 0): first}
    for near in (o, f):
        for over, up in ((0, 1), (0, 3), (1, 0)):
            near[over, up] = hop(near[0, 0], over, up)
    o[0, 2] = hop(o[0, 1], 0, 1)
    f[0, 2] = hop(f[0, 3], 0, 3)
    for near in (o, f):
        near[1, 1] = hop(near[1, 0], 0, 1)
        near[1, 3] = hop(near[1, 0], 0, 3)

    def picked(stage):
        spots = [(0, at) for at in stage] + [(1, at) for at in stage]
        return spots, [(f, o)[place][at] for place, at in spots]

    spots, blocks = picked(NEAR[:4])
    weights_in, weights_out, above, below = place_first(spots, blocks, (o[1, 1], f[1, 3]))
    o[1, 2] = hop(above, 0, 1)
    f[1, 2] = hop(below, 0, 3)
    return place_last(*picked(NEAR[4:]), token, weights_in, weights_out)


def place_of():
    half, plane = lax.axis_index("xh"), lax.axis_index("z")
    return jnp.where(half == 0, PLANES - 1 - plane, plane)


def working(step):
    order = step - SKEW * place_of()
    return (order >= 0) & (order < CHUNKS)


def project_kernel(step, u_ref, w_ref, *refs):
    out_ref = refs[-1]

    @pl.when(working(step))
    def _():
        out_ref[...] = dot(u_ref[...], w_ref[...], ((1,), (1,)))


def project_start_kernel(step, u_ref, chunk_ref, w_ref, *refs):
    out_ref, used_ref = refs[-2:]
    place = place_of()

    @pl.when(place == 0)
    def _():
        used_ref[...] = chunk_ref[...]

    @pl.when(place != 0)
    def _():
        used_ref[...] = u_ref[...]

    @pl.when(working(step))
    def _():
        out_ref[...] = dot(used_ref[...], w_ref[...], ((1,), (1,)))


def project(step, upstream, chunk, weights_out, tokens):
    if upstream is None:
        upstream, chunk = chunk, None
    rows, width = upstream.shape
    double = weights_out.shape[0]
    kernel, given = project_kernel, (upstream,)
    out = (jax.ShapeDtypeStruct((rows, double), F32),)
    if chunk is not None:
        kernel, given = project_start_kernel, (upstream, chunk)
        out += (jax.ShapeDtypeStruct((rows, width), BF),)
    found = pl.pallas_call(
        lambda *refs: kernel(step, *refs),
        out_shape=out,
        in_specs=[VMEM] * (len(given) + 1 + len(tokens)),
        out_specs=(VMEM,) * len(out),
        cost_estimate=SHORT,
        compiler_params=params(8),
    )(*given, weights_out, *tokens)
    return (found[0], upstream) if chunk is None else found


def relay_kernel(
    step, mine, other, u_ref, m_ref, rates_ref, w_ref, sg_hbm, u2_ref, token, sg, sem
):
    del token
    @pl.when(working(step))
    def _():
        state = m_ref.shape[0]
        grad = mine[...] + other[...]
        first = time_scan(grad[:, :state], rates_ref[0:1, :], True).astype(BF)
        sg[0] = first
        grad2 = grad[:, state:] + dot(first, m_ref[...], ((1,), (0,)))
        second = time_scan(grad2, rates_ref[1:2, :], True).astype(BF)
        sg[1] = second
        copy = pltpu.make_async_copy(sg, sg_hbm, sem)
        copy.start()
        width = u_ref.shape[1]
        tile = 512

        @pl.when(place_of() < PLANES - 1)
        def _():
            for at in range(0, width, tile):
                cols = pl.ds(at, tile)
                carried = dot(first, w_ref[0, cols, :], ((1,), (1,)))
                middle = (u_ref[:, cols].astype(F32) + carried).astype(BF)
                carried = dot(second, w_ref[1, cols, :], ((1,), (1,)))
                u2_ref[:, cols] = (middle.astype(F32) + carried).astype(BF)

        copy.wait()


def relay_step(step, mine, other, upstream, between, rates, weights_in):
    rows, width = upstream.shape
    state = between.shape[0]
    return pl.pallas_call(
        lambda *refs: relay_kernel(step, *refs),
        out_shape=(
            jax.ShapeDtypeStruct((2, rows, state), BF),
            jax.ShapeDtypeStruct((rows, width), BF),
            TOKEN,
        ),
        in_specs=[VMEM] * 6,
        out_specs=(ANY, VMEM, VMEM),
        scratch_shapes=[pltpu.VMEM((2, rows, state), BF), pltpu.SemaphoreType.DMA],
        cost_estimate=SHORT,
        compiler_params=params(8),
    )(mine, other, upstream, between, rates, weights_in)


def cut_kernel(first, second, cut_ref, token):
    del token
    count, _, _, part = cut_ref.shape
    for place, ref in enumerate((first, second)):
        for j in range(count):
            cut_ref[j, place] = ref[:, j * part : (j + 1) * part]


def cut_saved(first, second, count):
    rows, width = first.shape
    return pl.pallas_call(
        cut_kernel,
        out_shape=(jax.ShapeDtypeStruct((count, 2, rows, width // count), BF), TOKEN),
        in_specs=[VMEM] * 2,
        out_specs=(VMEM,) * 2,
        cost_estimate=SHORT,
        compiler_params=params(16),
    )(first, second)


def hidden_kernel(spot, *refs):
    rows, (w_ref, mine_ref, other_ref) = refs[:4], refs[4:]
    part = w_ref.shape[1] // len(NEAR)
    for core in range(2):

        @pl.when(spot[1] == core)
        def _():
            for n, ref in enumerate(rows):
                place, out_ref = n % 2, (mine_ref, other_ref)[n // 2]
                total = 0.0
                for i in range(len(NEAR)):
                    at = (2 * i + core) * part
                    weight = w_ref[place, i * part : (i + 1) * part, :]
                    total += dot(ref[:, at : at + part], weight, ((1,), (0,)))
                out_ref[place] = total


def hidden_parts(spot, first, own, others, weights_in):
    rows, _ = first.shape
    state = weights_in.shape[2]
    return pl.pallas_call(
        hidden_kernel,
        out_shape=(jax.ShapeDtypeStruct((2, rows, state), F32),) * 2,
        in_specs=[SMEM] + [VMEM] * 5,
        out_specs=(VMEM,) * 2,
        cost_estimate=SHORT,
        compiler_params=params(8),
    )(spot, first, own, others[0], others[1], weights_in)


def latent_kernel(mine, other, rates_ref, out_ref):
    for place in range(2):
        hidden = mine[place] + other[place]
        out_ref[place] = time_scan(hidden, rates_ref[place : place + 1, :], False).astype(BF)


def latents(mine, other, rates):
    return pl.pallas_call(
        latent_kernel,
        out_shape=jax.ShapeDtypeStruct(mine.shape, BF),
        in_specs=[VMEM] * 3,
        out_specs=VMEM,
        cost_estimate=SHORT,
        compiler_params=params(8),
    )(mine, other, rates)


def collect_kernel(steps, spot, latent, *refs):
    uppers, states = refs[:steps], refs[steps : 2 * steps]
    out_ref, upper, state, sems = refs[2 * steps :]
    chunks = CHUNKS
    chips, _, _, wide = out_ref.shape
    part = upper.shape[2] // chips
    width = state.shape[3]
    for t in range(PLANES):

        @pl.when(spot[2] == t)
        def _():
            copies = []
            for n in range(chunks):
                at = SKEW * t + n
                copies.append(pltpu.make_async_copy(uppers[at], upper.at[n], sems.at[n]))
                copies.append(pltpu.make_async_copy(states[at], state.at[n], sems.at[chunks + n]))
            for copy in copies:
                copy.start()
            for copy in copies:
                copy.wait()

    for n in range(chunks):
        own = state[2 * (n // 2) + spot[1], n % 2]
        rows = own.shape[0]
        own_latent = latent[n % 2, n // 2 * rows : (n // 2 + 1) * rows, :]
        for i in range(chips):
            out_ref[i, n, :, :part] = upper[n, :, i * part : (i + 1) * part]
            out_ref[i, n, :, wide - 2 * width : wide - width] = own
            out_ref[i, n, :, wide - width :] = own_latent


def collect(spot, latent, uppers, states, chips):
    steps, chunks = len(uppers), CHUNKS
    rows, width = uppers[0].shape
    state = states[0].shape[2]
    wide = lanes(width // chips) + 2 * state
    return pl.pallas_call(
        lambda *refs: collect_kernel(steps, *refs),
        out_shape=jax.ShapeDtypeStruct((chips, chunks, rows, wide), BF),
        in_specs=[SMEM, VMEM] + [ANY] * (2 * steps),
        out_specs=VMEM,
        scratch_shapes=[
            pltpu.VMEM((chunks, rows, width), BF),
            pltpu.VMEM((chunks, 2, rows, state), BF),
            pltpu.SemaphoreType.DMA((2 * chunks,)),
        ],
        cost_estimate=SHORT,
        compiler_params=params(16),
    )(spot, latent, *uppers, *states)


def gradient_kernel(
    spot, x_ref, relayed, others, w_ref, in_ref, out_ref, sum_in, sum_out
):
    part, state = in_ref.shape[1:]
    wide = relayed.shape[-1]
    group = relayed.shape[0]
    turn = pl.program_id(0)

    @pl.when(turn == 0)
    def _():
        sum_in[...] = jnp.zeros_like(sum_in)
        sum_out[...] = jnp.zeros_like(sum_out)

    def by_core(own, other):
        even = jnp.where(spot[1] == 0, own, other)
        odd = jnp.where(spot[1] == 0, other, own)
        return jnp.stack([even, odd], axis=1)

    micro = relayed.shape[1] // 2

    def rows_of(place, at):
        mine = relayed[:, :, :, wide - 2 * state + at : wide - state + at]
        theirs = others[:, :, :, at : at + state]
        return by_core(
            jnp.stack([mine[:, 2 * m + place] for m in range(micro)], axis=1),
            jnp.stack([theirs[:, 2 * m + place] for m in range(micro)], axis=1),
        ).reshape(-1, state)

    upper = relayed[:, :, :, :part]
    upper = jnp.stack(
        [jnp.stack([upper[:, 2 * m + r] for m in range(micro)], axis=1) for r in range(2)], axis=1
    ).reshape(-1, part)
    for place in range(2):
        grad, latent = rows_of(place, 0), rows_of(place, state)
        x = x_ref[:, place].reshape(-1, part)
        sum_in[place] += dot(x, grad, ((0,), (0,)))
        sum_out[place] += dot(latent, upper, ((0,), (0,)))
        if place == 0:
            carried = dot(grad, w_ref[...], ((1,), (1,)))
            upper = (upper.astype(F32) + carried).astype(BF)

    @pl.when(turn == pl.num_programs(0) - 1)
    def _():
        in_ref[...] = sum_in[...].astype(BF)
        out_ref[spot[0]] = sum_out[1].astype(BF)
        out_ref[1 - spot[0]] = sum_out[0].astype(BF)


def gradients(spot, x_all, relayed, others, weight):
    chips, chunks, rows, wide = relayed.shape
    part, state = weight.shape
    group = 2

    def blocks(array, count):
        rest = array.shape[1:]
        return pl.BlockSpec((count,) + rest, lambda i: (i,) + (0,) * len(rest))

    return pl.pallas_call(
        gradient_kernel,
        grid=(chips // group,),
        out_shape=(
            jax.ShapeDtypeStruct((2, part, state), BF),
            jax.ShapeDtypeStruct((2, state, part), BF),
        ),
        in_specs=[
            SMEM,
            blocks(x_all, 2 * group),
            blocks(relayed, group),
            blocks(others, group),
            pl.BlockSpec(weight.shape, lambda i: (0, 0)),
        ],
        out_specs=(
            pl.BlockSpec((2, part, state), lambda i: (0, 0, 0)),
            pl.BlockSpec((2, state, part), lambda i: (0, 0, 0)),
        ),
        scratch_shapes=[pltpu.VMEM((2, part, state), F32), pltpu.VMEM((2, state, part), F32)],
        cost_estimate=SHORT,
        compiler_params=params(24),
    )(spot, x_all, relayed, others, weight)


def after(block, other):
    return block + (other[(0,) * other.ndim].astype(F32) * 0.0).astype(block.dtype)


def on_device(saved_a, saved_b, cot_a, cot_b, w_in, w_out, decay_rate):
    plane, half, core = lax.axis_index("z"), lax.axis_index("xh"), lax.axis_index("core")
    chips = lax.axis_size(CHIPS)
    micro, length, width = saved_a.shape[1:]
    part = width // (2 * chips)
    state = w_in.shape[3]
    share = state // chips
    chunks = 2 * micro
    place = jnp.where(half == 0, PLANES - 1 - plane, plane)
    spot = jnp.stack([half, core, place]).astype(jnp.int32)

    def by_half(a, b):
        return jnp.where(half == 0, a, b)

    def by_core(a, b):
        return jnp.where(core == 0, a, b)

    def pair_rows(block, axis):
        even = jnp.concatenate(
            [block[..., 2 * i * part : (2 * i + 1) * part] for i in range(chips)], axis=-1
        )
        odd = jnp.concatenate(
            [block[..., (2 * i + 1) * part : (2 * i + 2) * part] for i in range(chips)], axis=-1
        )
        keep, got = by_core(even, odd), swap(by_core(odd, even), "core")
        return by_core(
            jnp.concatenate([keep, got], axis=axis), jnp.concatenate([got, keep], axis=axis)
        )

    shard_out = pair_rows(w_out[0], 1).reshape(2, share, width // (2 * state), state)
    shard_out = shard_out.transpose(0, 2, 1, 3).reshape(2, part, state)
    shard = jnp.concatenate([w_in[0], shard_out], axis=1)
    own = by_half(shard[0], shard[1])
    high = decay_rate[0].astype(BF)
    rest = decay_rate[0] - high.astype(F32)
    middle = rest.astype(BF)
    low = (rest - middle.astype(F32)).astype(BF)
    pieces = jnp.pad(jnp.stack([high, middle, low], axis=1), ((0, 0), (0, 13), (0, 0)))
    sent = jnp.concatenate([shard, pieces], axis=1)
    sent = lax.all_to_all(sent, "xh", 0, 0)
    sent = by_half(sent[1], sent[0])
    first, pieces = sent[: 2 * part], sent[2 * part : 2 * part + 3].astype(F32)
    first_rate = pieces[0] + pieces[1] + pieces[2]
    rates = jnp.stack([first_rate, by_half(decay_rate[0, 0], decay_rate[0, 1])])

    saved = lax.all_to_all(after(jnp.stack([saved_a[0], saved_b[0]]), first), "xh", 0, 0)
    saved_own = by_half(saved_a[0], saved_b[0]).reshape(micro * length, width)
    saved_first = by_half(saved[1], saved[0]).reshape(micro * length, width)
    saved_others = swap(jnp.stack([saved_first, saved_own]), "core")
    cut, cut_done = cut_saved(saved_first, saved_own, 2 * chips)
    x_all = lax.all_to_all(cut, DP, 0, 0)
    cot = pair_rows(by_half(cot_a, cot_b), 1).reshape(chunks, length, width // 2)

    weights_in, weights_out, between = gather_blocks(own, first, cut_done)
    between = (between + swap(between, "core")).astype(BF)

    steps = SKEW * (PLANES - 1) + chunks
    arriving, uppers, states = {}, [], []
    tokens = ()
    for step in range(steps):
        chunk = cot[step] if step < chunks else None
        part_grad, upstream = project(step, arriving.get(step), chunk, weights_out, tokens)
        state_grad, passing, token = relay_step(
            step, part_grad, swap(part_grad, "core"), upstream, between, rates, weights_in
        )
        uppers.append(upstream)
        states.append(state_grad)
        tokens = (token,)
        if step == 8:
            tokens += (x_all[0, 0, :8, :128],)
        route = []
        for at in range(PLANES - 1):
            if 0 <= step - SKEW * at < chunks:
                route.append(((PLANES - 1 - at) * 2, (PLANES - 2 - at) * 2))
                route.append((at * 2 + 1, (at + 1) * 2 + 1))
        if route:
            arriving[step + SKEW] = lax.ppermute(passing, SECTION, route)

    mine, other = hidden_parts(spot, saved_first, saved_own, saved_others, weights_in)
    latent = latents(mine, swap(other, "core"), rates)
    relayed = lax.all_to_all(collect(spot, latent, uppers, states, chips), CHIPS, 0, 0)
    others = swap(relayed[..., lanes(part) :], "core")
    grad_in, grad_out = gradients(spot, x_all, relayed, others, first[:part])
    other_in = swap(grad_in[0], "xh")
    grad_in = jnp.stack([by_half(grad_in[1], other_in), by_half(other_in, grad_in[1])])
    rows = state // (2 * chips)
    grad_out = lax.all_to_all(grad_out.reshape(4 * chips, rows, part), ("xh",) + DP, 0, 0)
    grad_out = grad_out.reshape(2, 2 * chips, rows, part).transpose(0, 2, 1, 3)
    grad_out = grad_out.reshape(2, rows, width)
    return grad_in.astype(F32)[None], grad_out.astype(F32)[None]


def solution(mesh):
    parts = Mesh(mesh.devices.reshape(PLANES, 2, 2, 4, 2), ("z", "xh", "xl", "y", "core"))
    rows = P(SECTION, None, DP, None)
    return jax.shard_map(
        on_device,
        mesh=parts,
        in_specs=(
            rows,
            rows,
            P(None, DP, None),
            P(None, DP, None),
            rows,
            rows,
            P(SECTION, None, None),
        ),
        out_specs=(rows, rows),
        check_vma=False,
    )
```

```python
import jax
import jax.numpy as jnp
from jax import lax
from jax.experimental import pallas as pl
from jax.experimental.pallas import tpu as pltpu
from jax.sharding import Mesh, PartitionSpec as P

SECTION = ("z", "xh")
CHIPS = ("xl", "y")
DP = ("xl", "y", "core")
PLANES = 8
SEQ = 32
CHUNKS = 4
SKEW = 2
SWAP = [(0, 1), (1, 0)]
BF, F32 = jnp.bfloat16, jnp.float32
SHORT = pl.CostEstimate(flops=1, bytes_accessed=1, transcendentals=0)
TOKEN = jax.ShapeDtypeStruct((8, 128), F32)
VMEM = pl.BlockSpec(memory_space=pltpu.VMEM)
SMEM = pl.BlockSpec(memory_space=pltpu.SMEM)
ANY = pl.BlockSpec(memory_space=pl.ANY)


def swap(block, axis):
    return lax.ppermute(block, axis, SWAP)


def dot(a, b, contract):
    return lax.dot_general(a, b, (contract, ((), ())), preferred_element_type=F32)


def params(mib):
    return pltpu.CompilerParams(vmem_limit_bytes=mib * 2**20)


def lanes(count):
    return -(-count // 128) * 128


def time_scan(values, rates, reverse):
    rows = values.shape[0]
    place = lax.broadcasted_iota(jnp.int32, values.shape, 0) % SEQ
    for step in (1, 2, 4, 8, 16):
        if reverse:
            moved = pltpu.roll(values, rows - step, 0)
            inside = place < SEQ - step
        else:
            moved = pltpu.roll(values, step, 0)
            inside = place >= step
        values = values + jnp.where(inside, moved, 0.0) * jnp.exp(-rates * step)
    return values


NEAR = ((0, 0), (0, 1), (0, 3), (1, 0), (0, 2), (1, 1), (1, 3), (1, 2))


def place_blocks(spots, blocks, w_in_ref, w_out_ref):
    depth, state = blocks[0].shape[0] // 2, blocks[0].shape[1]
    share = state // len(NEAR)
    xl, y = lax.axis_index("xl"), lax.axis_index("y")
    for (place, (over, up)), packed in zip(spots, blocks):
        i = lax.rem(xl + over, 2) * 4 + lax.rem(y + up, 4)
        at = pl.multiple_of(i * depth, depth)
        w_in_ref[place, pl.ds(at, depth), :] = packed[:depth, :]
        at = pl.multiple_of(place * state + i * share, share)
        for t in range(depth // share):
            w_out_ref[pl.ds(at, share), t * state : (t + 1) * state] = packed[
                depth + t * share : depth + (t + 1) * share, :
            ]


def place_first_kernel(spots, refs):
    blocks, passed = refs[: len(spots)], refs[len(spots) :][:2]
    w_in_ref, w_out_ref, *out = refs[len(spots) + 2 :]
    for block, ref in zip(passed, out):
        ref[...] = block[...]
    place_blocks(spots, blocks, w_in_ref, w_out_ref)


def place_first(spots, blocks, passed):
    depth, state = blocks[0].shape[0] // 2, blocks[0].shape[1]
    width = len(NEAR) * depth
    return pl.pallas_call(
        lambda *refs: place_first_kernel(spots, refs),
        out_shape=(
            jax.ShapeDtypeStruct((2, width, state), BF),
            jax.ShapeDtypeStruct((2 * state, width), BF),
        )
        + tuple(jax.ShapeDtypeStruct(block.shape, BF) for block in passed),
        in_specs=[VMEM] * (len(blocks) + 2),
        out_specs=(VMEM,) * 4,
        cost_estimate=SHORT,
        compiler_params=params(8),
    )(*blocks, *passed)


def place_last_kernel(spots, refs):
    blocks, (w_in_ref, w_out_ref, between_ref) = refs[: len(spots)], refs[-3:]
    place_blocks(spots, blocks, w_in_ref, w_out_ref)
    state = between_ref.shape[0]
    between_ref[...] = dot(w_in_ref[0], w_out_ref[state:, :], ((0,), (1,)))


def place_last(spots, blocks, token, weights_in, weights_out):
    state = weights_in.shape[2]
    count = len(blocks) + 1
    return pl.pallas_call(
        lambda *refs: place_last_kernel(spots, refs),
        out_shape=(
            jax.ShapeDtypeStruct(weights_in.shape, BF),
            jax.ShapeDtypeStruct(weights_out.shape, BF),
            jax.ShapeDtypeStruct((state, state), F32),
        ),
        in_specs=[VMEM] * (count + 2),
        out_specs=(VMEM,) * 3,
        input_output_aliases={count: 0, count + 1: 1},
        cost_estimate=SHORT,
        compiler_params=params(8),
    )(*blocks, token, weights_in, weights_out)


def gather_blocks(own, first, token):
    def hop(block, over, up):
        route = [
            (x * 4 + y, (x + over) % 2 * 4 + (y - up) % 4) for x in range(2) for y in range(4)
        ]
        return lax.ppermute(block, CHIPS, route)

    o, f = {(0, 0): own}, {(0, 0): first}
    for near in (o, f):
        for over, up in ((0, 1), (0, 3), (1, 0)):
            near[over, up] = hop(near[0, 0], over, up)
    o[0, 2] = hop(o[0, 1], 0, 1)
    f[0, 2] = hop(f[0, 3], 0, 3)
    for near in (o, f):
        near[1, 1] = hop(near[1, 0], 0, 1)
        near[1, 3] = hop(near[1, 0], 0, 3)

    def picked(stage):
        spots = [(0, at) for at in stage] + [(1, at) for at in stage]
        return spots, [(f, o)[place][at] for place, at in spots]

    spots, blocks = picked(NEAR[:4])
    weights_in, weights_out, above, below = place_first(spots, blocks, (o[1, 1], f[1, 3]))
    o[1, 2] = hop(above, 0, 1)
    f[1, 2] = hop(below, 0, 3)
    return place_last(*picked(NEAR[4:]), token, weights_in, weights_out)


def place_of():
    half, plane = lax.axis_index("xh"), lax.axis_index("z")
    return jnp.where(half == 0, PLANES - 1 - plane, plane)


def working(step):
    order = step - SKEW * place_of()
    return (order >= 0) & (order < CHUNKS)


def project_kernel(step, u_ref, w_ref, *refs):
    out_ref = refs[-1]

    @pl.when(working(step))
    def _():
        out_ref[...] = dot(u_ref[...], w_ref[...], ((1,), (1,)))


def project_start_kernel(step, u_ref, chunk_ref, w_ref, *refs):
    out_ref, used_ref = refs[-2:]
    place = place_of()

    @pl.when(place == 0)
    def _():
        used_ref[...] = chunk_ref[...]

    @pl.when(place != 0)
    def _():
        used_ref[...] = u_ref[...]

    @pl.when(working(step))
    def _():
        out_ref[...] = dot(used_ref[...], w_ref[...], ((1,), (1,)))


def project(step, upstream, chunk, weights_out, tokens):
    if upstream is None:
        upstream, chunk = chunk, None
    rows, width = upstream.shape
    double = weights_out.shape[0]
    kernel, given = project_kernel, (upstream,)
    out = (jax.ShapeDtypeStruct((rows, double), F32),)
    if chunk is not None:
        kernel, given = project_start_kernel, (upstream, chunk)
        out += (jax.ShapeDtypeStruct((rows, width), BF),)
    found = pl.pallas_call(
        lambda *refs: kernel(step, *refs),
        out_shape=out,
        in_specs=[VMEM] * (len(given) + 1 + len(tokens)),
        out_specs=(VMEM,) * len(out),
        cost_estimate=SHORT,
        compiler_params=params(8),
    )(*given, weights_out, *tokens)
    return (found[0], upstream) if chunk is None else found


def relay_kernel(
    step, mine, other, u_ref, m_ref, rates_ref, w_ref, sg_hbm, u2_ref, token, sg, sem
):
    del token
    @pl.when(working(step))
    def _():
        state = m_ref.shape[0]
        grad = mine[...] + other[...]
        first = time_scan(grad[:, :state], rates_ref[0:1, :], True).astype(BF)
        sg[0] = first
        grad2 = grad[:, state:] + dot(first, m_ref[...], ((1,), (0,)))
        second = time_scan(grad2, rates_ref[1:2, :], True).astype(BF)
        sg[1] = second
        copy = pltpu.make_async_copy(sg, sg_hbm, sem)
        copy.start()
        width = u_ref.shape[1]
        tile = 512

        @pl.when(place_of() < PLANES - 1)
        def _():
            for at in range(0, width, tile):
                cols = pl.ds(at, tile)
                carried = dot(first, w_ref[0, cols, :], ((1,), (1,)))
                middle = (u_ref[:, cols].astype(F32) + carried).astype(BF)
                carried = dot(second, w_ref[1, cols, :], ((1,), (1,)))
                u2_ref[:, cols] = (middle.astype(F32) + carried).astype(BF)

        copy.wait()


def relay_step(step, mine, other, upstream, between, rates, weights_in):
    rows, width = upstream.shape
    state = between.shape[0]
    return pl.pallas_call(
        lambda *refs: relay_kernel(step, *refs),
        out_shape=(
            jax.ShapeDtypeStruct((2, rows, state), BF),
            jax.ShapeDtypeStruct((rows, width), BF),
            TOKEN,
        ),
        in_specs=[VMEM] * 6,
        out_specs=(ANY, VMEM, VMEM),
        scratch_shapes=[pltpu.VMEM((2, rows, state), BF), pltpu.SemaphoreType.DMA],
        cost_estimate=SHORT,
        compiler_params=params(8),
    )(mine, other, upstream, between, rates, weights_in)


def cut_kernel(first, second, cut_ref, token):
    del token
    count, _, _, part = cut_ref.shape
    for place, ref in enumerate((first, second)):
        for j in range(count):
            cut_ref[j, place] = ref[:, j * part : (j + 1) * part]


def cut_saved(first, second, count):
    rows, width = first.shape
    return pl.pallas_call(
        cut_kernel,
        out_shape=(jax.ShapeDtypeStruct((count, 2, rows, width // count), BF), TOKEN),
        in_specs=[VMEM] * 2,
        out_specs=(VMEM,) * 2,
        cost_estimate=SHORT,
        compiler_params=params(16),
    )(first, second)


def hidden_kernel(spot, *refs):
    rows, (w_ref, mine_ref, other_ref) = refs[:4], refs[4:]
    part = w_ref.shape[1] // len(NEAR)
    for core in range(2):

        @pl.when(spot[1] == core)
        def _():
            for n, ref in enumerate(rows):
                place, out_ref = n % 2, (mine_ref, other_ref)[n // 2]
                total = 0.0
                for i in range(len(NEAR)):
                    at = (2 * i + core) * part
                    weight = w_ref[place, i * part : (i + 1) * part, :]
                    total += dot(ref[:, at : at + part], weight, ((1,), (0,)))
                out_ref[place] = total


def hidden_parts(spot, first, own, others, weights_in):
    rows, _ = first.shape
    state = weights_in.shape[2]
    return pl.pallas_call(
        hidden_kernel,
        out_shape=(jax.ShapeDtypeStruct((2, rows, state), F32),) * 2,
        in_specs=[SMEM] + [VMEM] * 5,
        out_specs=(VMEM,) * 2,
        cost_estimate=SHORT,
        compiler_params=params(8),
    )(spot, first, own, others[0], others[1], weights_in)


def latent_kernel(mine, other, rates_ref, out_ref):
    for place in range(2):
        hidden = mine[place] + other[place]
        out_ref[place] = time_scan(hidden, rates_ref[place : place + 1, :], False).astype(BF)


def latents(mine, other, rates):
    return pl.pallas_call(
        latent_kernel,
        out_shape=jax.ShapeDtypeStruct(mine.shape, BF),
        in_specs=[VMEM] * 3,
        out_specs=VMEM,
        cost_estimate=SHORT,
        compiler_params=params(8),
    )(mine, other, rates)


def collect_kernel(steps, spot, latent, *refs):
    uppers, states = refs[:steps], refs[steps : 2 * steps]
    out_ref, upper, state, sems = refs[2 * steps :]
    chunks = CHUNKS
    chips, _, _, wide = out_ref.shape
    part = upper.shape[2] // chips
    width = state.shape[3]
    for t in range(PLANES):

        @pl.when(spot[2] == t)
        def _():
            copies = []
            for n in range(chunks):
                at = SKEW * t + n
                copies.append(pltpu.make_async_copy(uppers[at], upper.at[n], sems.at[n]))
                copies.append(pltpu.make_async_copy(states[at], state.at[n], sems.at[chunks + n]))
            for copy in copies:
                copy.start()
            for copy in copies:
                copy.wait()

    for n in range(chunks):
        own = state[2 * (n // 2) + spot[1], n % 2]
        rows = own.shape[0]
        own_latent = latent[n % 2, n // 2 * rows : (n // 2 + 1) * rows, :]
        for i in range(chips):
            out_ref[i, n, :, :part] = upper[n, :, i * part : (i + 1) * part]
            out_ref[i, n, :, wide - 2 * width : wide - width] = own
            out_ref[i, n, :, wide - width :] = own_latent


def collect(spot, latent, uppers, states, chips):
    steps, chunks = len(uppers), CHUNKS
    rows, width = uppers[0].shape
    state = states[0].shape[2]
    wide = lanes(width // chips) + 2 * state
    return pl.pallas_call(
        lambda *refs: collect_kernel(steps, *refs),
        out_shape=jax.ShapeDtypeStruct((chips, chunks, rows, wide), BF),
        in_specs=[SMEM, VMEM] + [ANY] * (2 * steps),
        out_specs=VMEM,
        scratch_shapes=[
            pltpu.VMEM((chunks, rows, width), BF),
            pltpu.VMEM((chunks, 2, rows, state), BF),
            pltpu.SemaphoreType.DMA((2 * chunks,)),
        ],
        cost_estimate=SHORT,
        compiler_params=params(16),
    )(spot, latent, *uppers, *states)


def gradient_kernel(
    spot, x_ref, relayed, others, w_ref, in_ref, out_ref, sum_in, sum_out
):
    part, state = in_ref.shape[1:]
    wide = relayed.shape[-1]
    group = relayed.shape[0]
    turn = pl.program_id(0)

    @pl.when(turn == 0)
    def _():
        sum_in[...] = jnp.zeros_like(sum_in)
        sum_out[...] = jnp.zeros_like(sum_out)

    def by_core(own, other):
        even = jnp.where(spot[1] == 0, own, other)
        odd = jnp.where(spot[1] == 0, other, own)
        return jnp.stack([even, odd], axis=1)

    micro = relayed.shape[1] // 2

    def rows_of(place, at):
        mine = relayed[:, :, :, wide - 2 * state + at : wide - state + at]
        theirs = others[:, :, :, at : at + state]
        return by_core(
            jnp.stack([mine[:, 2 * m + place] for m in range(micro)], axis=1),
            jnp.stack([theirs[:, 2 * m + place] for m in range(micro)], axis=1),
        ).reshape(-1, state)

    upper = relayed[:, :, :, :part]
    upper = jnp.stack(
        [jnp.stack([upper[:, 2 * m + r] for m in range(micro)], axis=1) for r in range(2)], axis=1
    ).reshape(-1, part)
    for place in range(2):
        grad, latent = rows_of(place, 0), rows_of(place, state)
        x = x_ref[:, place].reshape(-1, part)
        sum_in[place] += dot(x, grad, ((0,), (0,)))
        sum_out[place] += dot(latent, upper, ((0,), (0,)))
        if place == 0:
            carried = dot(grad, w_ref[...], ((1,), (1,)))
            upper = (upper.astype(F32) + carried).astype(BF)

    @pl.when(turn == pl.num_programs(0) - 1)
    def _():
        in_ref[...] = sum_in[...].astype(BF)
        out_ref[spot[0]] = sum_out[1].astype(BF)
        out_ref[1 - spot[0]] = sum_out[0].astype(BF)


def gradients(spot, x_all, relayed, others, weight):
    chips, chunks, rows, wide = relayed.shape
    part, state = weight.shape
    group = 4

    def blocks(array, count):
        rest = array.shape[1:]
        return pl.BlockSpec((count,) + rest, lambda i: (i,) + (0,) * len(rest))

    return pl.pallas_call(
        gradient_kernel,
        grid=(chips // group,),
        out_shape=(
            jax.ShapeDtypeStruct((2, part, state), BF),
            jax.ShapeDtypeStruct((2, state, part), BF),
        ),
        in_specs=[
            SMEM,
            blocks(x_all, 2 * group),
            blocks(relayed, group),
            blocks(others, group),
            pl.BlockSpec(weight.shape, lambda i: (0, 0)),
        ],
        out_specs=(
            pl.BlockSpec((2, part, state), lambda i: (0, 0, 0)),
            pl.BlockSpec((2, state, part), lambda i: (0, 0, 0)),
        ),
        scratch_shapes=[pltpu.VMEM((2, part, state), F32), pltpu.VMEM((2, state, part), F32)],
        cost_estimate=SHORT,
        compiler_params=params(24),
    )(spot, x_all, relayed, others, weight)


def after(block, other):
    return block + (other[(0,) * other.ndim].astype(F32) * 0.0).astype(block.dtype)


def on_device(saved_a, saved_b, cot_a, cot_b, w_in, w_out, decay_rate):
    plane, half, core = lax.axis_index("z"), lax.axis_index("xh"), lax.axis_index("core")
    chips = lax.axis_size(CHIPS)
    micro, length, width = saved_a.shape[1:]
    part = width // (2 * chips)
    state = w_in.shape[3]
    share = state // chips
    chunks = 2 * micro
    place = jnp.where(half == 0, PLANES - 1 - plane, plane)
    spot = jnp.stack([half, core, place]).astype(jnp.int32)

    def by_half(a, b):
        return jnp.where(half == 0, a, b)

    def by_core(a, b):
        return jnp.where(core == 0, a, b)

    def pair_rows(block, axis):
        even = jnp.concatenate(
            [block[..., 2 * i * part : (2 * i + 1) * part] for i in range(chips)], axis=-1
        )
        odd = jnp.concatenate(
            [block[..., (2 * i + 1) * part : (2 * i + 2) * part] for i in range(chips)], axis=-1
        )
        keep, got = by_core(even, odd), swap(by_core(odd, even), "core")
        return by_core(
            jnp.concatenate([keep, got], axis=axis), jnp.concatenate([got, keep], axis=axis)
        )

    shard_out = pair_rows(w_out[0], 1).reshape(2, share, width // (2 * state), state)
    shard_out = shard_out.transpose(0, 2, 1, 3).reshape(2, part, state)
    shard = jnp.concatenate([w_in[0], shard_out], axis=1)
    own = by_half(shard[0], shard[1])
    high = decay_rate[0].astype(BF)
    rest = decay_rate[0] - high.astype(F32)
    middle = rest.astype(BF)
    low = (rest - middle.astype(F32)).astype(BF)
    pieces = jnp.pad(jnp.stack([high, middle, low], axis=1), ((0, 0), (0, 13), (0, 0)))
    sent = jnp.concatenate([shard, pieces], axis=1)
    sent = lax.all_to_all(sent, "xh", 0, 0)
    sent = by_half(sent[1], sent[0])
    first, pieces = sent[: 2 * part], sent[2 * part : 2 * part + 3].astype(F32)
    first_rate = pieces[0] + pieces[1] + pieces[2]
    rates = jnp.stack([first_rate, by_half(decay_rate[0, 0], decay_rate[0, 1])])

    saved = lax.all_to_all(after(jnp.stack([saved_a[0], saved_b[0]]), first), "xh", 0, 0)
    saved_own = by_half(saved_a[0], saved_b[0]).reshape(micro * length, width)
    saved_first = by_half(saved[1], saved[0]).reshape(micro * length, width)
    saved_others = swap(jnp.stack([saved_first, saved_own]), "core")
    cut, cut_done = cut_saved(saved_first, saved_own, 2 * chips)
    x_all = lax.all_to_all(cut, DP, 0, 0)
    cot = pair_rows(by_half(cot_a, cot_b), 1).reshape(chunks, length, width // 2)

    weights_in, weights_out, between = gather_blocks(own, first, cut_done)
    between = (between + swap(between, "core")).astype(BF)

    steps = SKEW * (PLANES - 1) + chunks
    arriving, uppers, states = {}, [], []
    tokens = ()
    for step in range(steps):
        chunk = cot[step] if step < chunks else None
        part_grad, upstream = project(step, arriving.get(step), chunk, weights_out, tokens)
        state_grad, passing, token = relay_step(
            step, part_grad, swap(part_grad, "core"), upstream, between, rates, weights_in
        )
        uppers.append(upstream)
        states.append(state_grad)
        tokens = (token,)
        if step == 10:
            tokens += (x_all[0, 0, :8, :128],)
        route = []
        for at in range(PLANES - 1):
            if 0 <= step - SKEW * at < chunks:
                route.append(((PLANES - 1 - at) * 2, (PLANES - 2 - at) * 2))
                route.append((at * 2 + 1, (at + 1) * 2 + 1))
        if route:
            arriving[step + SKEW] = lax.ppermute(passing, SECTION, route)

    mine, other = hidden_parts(spot, saved_first, saved_own, saved_others, weights_in)
    latent = latents(mine, swap(other, "core"), rates)
    relayed = lax.all_to_all(collect(spot, latent, uppers, states, chips), CHIPS, 0, 0)
    others = swap(relayed[..., lanes(part) :], "core")
    grad_in, grad_out = gradients(spot, x_all, relayed, others, first[:part])
    other_in = swap(grad_in[0], "xh")
    grad_in = jnp.stack([by_half(grad_in[1], other_in), by_half(other_in, grad_in[1])])
    rows = state // (2 * chips)
    grad_out = lax.all_to_all(grad_out.reshape(4 * chips, rows, part), ("xh",) + DP, 0, 0)
    grad_out = grad_out.reshape(2, 2 * chips, rows, part).transpose(0, 2, 1, 3)
    grad_out = grad_out.reshape(2, rows, width)
    return grad_in.astype(F32)[None], grad_out.astype(F32)[None]


def solution(mesh):
    parts = Mesh(mesh.devices.reshape(PLANES, 2, 2, 4, 2), ("z", "xh", "xl", "y", "core"))
    rows = P(SECTION, None, DP, None)
    return jax.shard_map(
        on_device,
        mesh=parts,
        in_specs=(
            rows,
            rows,
            P(None, DP, None),
            P(None, DP, None),
            rows,
            rows,
            P(SECTION, None, None),
        ),
        out_specs=(rows, rows),
        check_vma=False,
    )
```
